768 devices in a mesh: ab: 48 (over z_lo, x, core), cd: 16 (over y, z_hi).
Axes of the slice: x: 4, y: 8, z: 12 (z_hi: 2, z_lo: 6; z = z_hi * 6 + z_lo), core: 2. Of those that a mesh axis runs over, the one named last changes fastest.
Arguments:
- integrals: bfloat16 [73728, 20480], P('ab', 'cd'), may hold values from -0.3125 to 0.3125
- tile_mask: int32 [288, 80], P('ab', 'cd'), may hold values 0 or 1
- virt_irrep: int32 [1000], replicated, may hold values from 0 to 7
- occ_pairs: int32 [2, 288], replicated, may hold values from 0 to 99
- virt_energy: float32 [1000], replicated, may hold values from 0.3 to 3
- occ_energy: float32 [100], replicated, may hold values from -2 to -0.5
- amp_ab: bfloat16 [288, 73728], P('cd', 'ab'), may hold values from -8 to 8
- amp_cd: bfloat16 [288, 20480], P('ab', 'cd'), may hold values from -8 to 8
Outputs:
- update_ab: float32 [288, 73728], P('cd', 'ab')
- update_cd: float32 [288, 20480], P('ab', 'cd')
The draws below stay inside these ranges and needn't reach their ends.
All inputs are finite; a program needn't handle non-finite values. No bound on the sum of `tile_mask` on one device may be relied on, other than what follows from the above.
Results may differ from the reference program's by a relative error of at most 0.0003.
Values may be sent and summed in bfloat16 or wider, within the bound.
No kernel may reach another device: no remote copies, remote signals or barrier semaphores. Data moves between devices by JAX's collectives and lax.ppermute only.
A program may use at most 32 MiB of HBM per device.

```python
import math
import jax
import jax.numpy as jnp
from jax import lax

NV = 1000
NOCC = 100
TILE = 256
PA_DEV = 1536
NPAIR = 288
NAB = 73728
NCD = 20480


def set_ends(array, stream_key, least, largest):
    dims = array.shape
    spot = [jax.random.randint(jax.random.fold_in(stream_key, axis), (), 0, dims[axis]) for axis in range(len(dims))]
    array = array.at[tuple(spot)].set(least)
    longest = dims.index(max(dims))
    spot[longest] = (spot[longest] + 1) % dims[longest]
    return array.at[tuple(spot)].set(largest)


def spiked(result, stream_key, source, target, blocks, factor):
    def block_of(position):
        return (jnp.arange(result.shape[position]) // (result.shape[position] // blocks)).reshape((-1,) + (1,) * (result.ndim - 1 - position))

    one_side = jax.random.permutation(stream_key, blocks)[block_of(target)]
    other_side = (block_of(target) + blocks // 2) % blocks
    return jnp.where((block_of(source) == one_side) | (block_of(source) == other_side), factor * result, result)


def steps_of(own_key, dims, cuts, least, high):
    gain = 1.0
    for position, blocks in cuts:
        draws = jax.random.uniform(jax.random.fold_in(jax.random.fold_in(own_key, 6), position), (blocks,), jnp.float32, least / len(cuts), high / len(cuts))
        gain = gain * jnp.repeat(jnp.exp(draws), dims[position] // blocks).reshape((-1,) + (1,) * (len(dims) - 1 - position))
    return gain


def centred(key, extent, width, most, split=(), held_as=jnp.bfloat16):
    loudness = steps_of(key, extent, split, -0.22, 0.18) if split else 1.0
    array = jax.random.normal(key, extent, jnp.float32) * width * loudness
    return jnp.minimum(jnp.maximum(array, -most), most).astype(held_as)


def heavy_noise(own_key, extent, width, most, pieces, heavy, kind=jnp.bfloat16):
    array = width * jax.random.normal(own_key, extent, jnp.float32)
    if pieces:
        array = array * steps_of(own_key, extent, pieces, -0.22, 0.18)
    return jnp.clip(spiked(array, jax.random.fold_in(own_key, 3), *heavy), -most, most).astype(kind)


def setup_inputs(seed: int = 0) -> dict:
    keys = jax.random.split(jax.random.key(seed), 9)
    return {
        "integrals": centred(keys[0], (NAB, NCD), (NCD // 64) ** -0.5, 0.3125, ((0, 48), (1, 16))),
        "tile_mask": set_ends((jax.random.randint(keys[1], (NAB // TILE, NCD // TILE), 0, 2) < 1).astype(jnp.int32), jax.random.fold_in(keys[1], 1), 0, 1),
        "virt_irrep": set_ends(jax.random.randint(keys[2], (NV,), 0, 8), jax.random.fold_in(keys[2], 1), 0, 7).astype(jnp.int32),
        "occ_pairs": set_ends(jax.random.randint(keys[3], (2, NPAIR), 0, NOCC), jax.random.fold_in(keys[3], 1), 0, NOCC - 1).astype(jnp.int32),
        "virt_energy": jnp.clip(jnp.exp(jax.random.uniform(keys[4], (NV,), jnp.float32, math.log(0.3), math.log(3.0))), 0.3, 3.0),
        "occ_energy": jnp.clip(jax.random.uniform(keys[5], (NOCC,), jnp.float32, -2.0, -0.5), -2.0, -0.5),
        "amp_ab": heavy_noise(keys[6], (NPAIR, NAB), 1.0, 8.0, ((0, 16), (1, 48)), (1, 0, 48, 3.25)),
        "amp_cd": centred(keys[7], (NPAIR, NCD), 1.0, 8.0, ((0, 48), (1, 16))),
    }


def pair_data(first, count, virt_irrep, virt_energy):
    index = first + jnp.arange(count, dtype=jnp.int32)
    left = index // NV
    right = index % NV
    irreps = jnp.bitwise_xor(virt_irrep[left], virt_irrep[right])
    energy = virt_energy[left] + virt_energy[right]
    return irreps, energy


def reference(integrals, tile_mask, virt_irrep, occ_pairs, virt_energy, occ_energy, amp_ab, amp_cd):
    nab = integrals.shape[0]
    ncd = integrals.shape[1]
    blocks = nab // PA_DEV
    col_irrep, col_energy = pair_data(nab, ncd, virt_irrep, virt_energy)
    occ_sum = occ_energy[occ_pairs[0]] + occ_energy[occ_pairs[1]]

    def step(carry, block):
        first = (block * PA_DEV).astype(jnp.int32)
        rows = lax.dynamic_slice_in_dim(integrals, first, PA_DEV, 0)
        tiles = lax.dynamic_slice_in_dim(tile_mask, (first // TILE).astype(jnp.int32), PA_DEV // TILE, 0)
        tiles = jnp.repeat(jnp.repeat(tiles, TILE, axis=0), TILE, axis=1)
        row_irrep, row_energy = pair_data(first, PA_DEV, virt_irrep, virt_energy)
        keep = (tiles == 1) & (row_irrep[:, None] == col_irrep[None, :])
        masked = jnp.where(keep, rows, jnp.zeros_like(rows))
        ladder_ab = lax.dot_general(amp_cd, masked, (((1,), (1,)), ((), ())), preferred_element_type=jnp.float32)
        amp_rows = lax.dynamic_slice_in_dim(amp_ab, first, PA_DEV, 1)
        carry = carry + jnp.dot(amp_rows, masked, preferred_element_type=jnp.float32)
        update = ladder_ab / (row_energy[None, :] - occ_sum[:, None])
        return carry, update

    start = jnp.zeros((amp_cd.shape[0], ncd), jnp.float32)
    ladder_cd, updates = lax.scan(step, start, jnp.arange(blocks, dtype=jnp.int32))
    update_ab = jnp.transpose(updates, (1, 0, 2)).reshape(amp_ab.shape[0], nab)
    update_cd = ladder_cd / (col_energy[None, :] - occ_sum[:, None])
    return update_ab, update_cd
```

```python
import jax
import jax.numpy as jnp
from jax import lax
from jax.sharding import Mesh
from jax.sharding import PartitionSpec as P

NV = 1000
TILE = 256
AB = ("zl", "x", "core")
CD = ("y", "zh")


def lookup(index, table):
    equal = index[:, None] == jnp.arange(table.shape[0], dtype=jnp.int32)[None, :]
    return jnp.sum(jnp.where(equal, table[None, :], jnp.zeros_like(table)[None, :]), axis=1)


def pair_data(first, count, virt_irrep, virt_energy):
    index = first + jnp.arange(count, dtype=jnp.int32)
    left = index // NV
    right = index % NV
    irreps = jnp.bitwise_xor(lookup(left, virt_irrep), lookup(right, virt_irrep))
    energy = lookup(left, virt_energy) + lookup(right, virt_energy)
    return (irreps, energy)


def occ_sums(occ_pairs, occ_energy, first, count):
    left = lax.dynamic_slice_in_dim(occ_pairs[0], first, count, 0)
    right = lax.dynamic_slice_in_dim(occ_pairs[1], first, count, 0)
    return lookup(left, occ_energy) + lookup(right, occ_energy)


def send(block, axis, size, shift):
    return lax.ppermute(block, axis, [(i, (i + shift) % size) for i in range(size)])


def pick(source, rows):
    chosen = (rows[:, None] == jnp.arange(source.shape[0], dtype=jnp.int32)[None, :]).astype(source.dtype)
    return jnp.dot(chosen, source, preferred_element_type=jnp.float32).astype(source.dtype)


def pad_rows(block, count):
    return jnp.pad(block, ((0, count - block.shape[0]), (0, 0)))


def local(integrals, tile_mask, virt_irrep, occ_pairs, virt_energy, occ_energy, amp_ab, amp_cd):
    rows_dev = integrals.shape[0]
    cols_dev = integrals.shape[1]
    nzl, nx, ncore, ny, nzh = (lax.axis_size(a) for a in ("zl", "x", "core", "y", "zh"))
    zl, x, core, y, zh = (lax.axis_index(a) for a in ("zl", "x", "core", "y", "zh"))
    row_group = (zl * nx + x) * ncore + core
    col_group = y * nzh + zh
    nab = rows_dev * nzl * nx * ncore
    cd_count = amp_cd.shape[0]
    ab_count = amp_ab.shape[0]
    npair = cd_count * nzl * nx * ncore

    own = pad_rows(amp_cd, 8)
    part = jnp.concatenate([own] + [send(own, "zl", nzl, -s) for s in range(1, nzl)], axis=0)
    part = jnp.concatenate([part] + [send(part, "x", nx, -t) for t in range(1, nx)], axis=0)
    all_cd = jnp.concatenate([part, send(part, "core", ncore, 1)], axis=0)

    own = jnp.concatenate([amp_ab, send(amp_ab, "zh", nzh, 1)], axis=0)
    block = 40
    own = pad_rows(own, block)
    pieces = {0: own}
    up = down = own
    for step in range(1, ny // 2):
        up = send(up, "y", ny, 1)
        down = send(down, "y", ny, -1)
        pieces[ny - step] = up
        pieces[step] = down
    half = block // 2
    pieces[ny // 2] = jnp.concatenate([send(up[:24], "y", ny, 1), send(down[24:], "y", ny, -1)], axis=0)
    all_ab = jnp.concatenate([pieces[d] for d in range(ny)], axis=0)

    row_first = row_group * rows_dev
    col_first = nab + col_group * cols_dev
    row_irrep, row_energy = pair_data(row_first, rows_dev, virt_irrep, virt_energy)
    col_irrep, col_energy = pair_data(col_first, cols_dev, virt_irrep, virt_energy)
    tiles = jnp.repeat(jnp.repeat(tile_mask, TILE, axis=0), TILE, axis=1)
    keep = (tiles == 1) & (row_irrep[:, None] == col_irrep[None, :])
    masked = jnp.where(keep, integrals, jnp.zeros_like(integrals))

    out = jnp.arange(npair, dtype=jnp.int32)
    chunk = nzh * ab_count
    k = ((y + out // chunk) % ny) * chunk + out % chunk
    group = k // cd_count
    z_off = (group // (nx * ncore) - zl) % nzl
    x_off = ((group // ncore) % nx - x) % nx
    core_off = (group % ncore - core) % ncore
    amp = pick(all_cd, ((core_off * nx + x_off) * nzl + z_off) * 8 + k % cd_count)
    partial_ab = lax.dot_general(amp, masked, (((1,), (1,)), ((), ())), preferred_element_type=jnp.float32)
    partial_ab = partial_ab.reshape(ny, nzh, ab_count, rows_dev)

    r = out % cd_count
    s = (out // cd_count) % nzl
    t = (out // (cd_count * nzl)) % nx
    u = out // (cd_count * nzl * nx)
    k = ((((zl + s) % nzl) * nx + (x + t) % nx) * ncore + (core + u) % ncore) * cd_count + r
    group = k // ab_count
    amp = pick(all_ab, ((group // nzh - y) % ny) * block + ((group % nzh - zh) % nzh) * ab_count + k % ab_count)
    partial_cd = jnp.dot(amp, masked, preferred_element_type=jnp.float32)

    up = send(partial_ab[ny // 2, 0], "y", ny, 1)
    down = send(partial_ab[ny // 2, 1], "y", ny, -1)
    mine = partial_ab[ny // 2 - 1]
    up = jnp.stack([mine[0] + up, mine[1]])
    mine = partial_ab[ny // 2 + 1]
    down = jnp.stack([mine[0], mine[1] + down])
    for step in range(ny // 2 - 1, 0, -1):
        up = send(up, "y", ny, 1) + partial_ab[step - 1]
        down = send(down, "y", ny, -1)
        if step > 1:
            down = down + partial_ab[ny - step + 1]
    total = up + down
    keep_half = lax.dynamic_index_in_dim(total, zh, 0, keepdims=False)
    give_half = lax.dynamic_index_in_dim(total, 1 - zh, 0, keepdims=False)
    ladder_ab = keep_half + send(give_half, "zh", nzh, 1)

    per_core = npair // ncore
    total = partial_cd[:per_core] + send(partial_cd[per_core:], "core", ncore, 1)
    total = total.reshape(nx, nzl * cd_count, cols_dev)
    total = total[0] + sum(send(total[t], "x", nx, t) for t in range(1, nx))
    total = total.reshape(nzl, cd_count, cols_dev)
    ladder_cd = total[0] + sum(send(total[s], "zl", nzl, s) for s in range(1, nzl))

    occ_ab = occ_sums(occ_pairs, occ_energy, col_group * ab_count, ab_count)
    occ_cd = occ_sums(occ_pairs, occ_energy, row_group * cd_count, cd_count)
    update_ab = ladder_ab / (row_energy[None, :] - occ_ab[:, None])
    update_cd = ladder_cd / (col_energy[None, :] - occ_cd[:, None])
    return (update_ab, update_cd)


def solution(mesh):
    fine = Mesh(mesh.devices.reshape(6, 4, 2, 8, 2), AB + CD)
    return jax.shard_map(
        local,
        mesh=fine,
        in_specs=(P(AB, CD), P(AB, CD), P(), P(), P(), P(), P(CD, AB), P(AB, CD)),
        out_specs=(P(CD, AB), P(AB, CD)),
        check_vma=False,
    )
```

```python
import jax
import jax.numpy as jnp
from jax import lax
from jax.sharding import Mesh
from jax.sharding import PartitionSpec as P

NV = 1000
TILE = 256
AB = ("zl", "x", "core")
CD = ("y", "zh")


def window(table, first, count):
    spans = (count + NV - 1) // NV + 1
    start = first % NV
    heads = lax.dynamic_slice_in_dim(table, first // NV, spans, 0)
    step = (start + jnp.arange(count, dtype=jnp.int32)) // NV
    left = jnp.where(step == 0, heads[0], heads[spans - 1])
    for j in range(1, spans - 1):
        left = jnp.where(step == j, heads[j], left)
    right = lax.dynamic_slice_in_dim(jnp.concatenate([table] * (spans + 1)), start, count, 0)
    return left, right


def send(block, axis, pairs):
    return lax.ppermute(block, axis, pairs)


def shift(size, by):
    return [(i, (i + by) % size) for i in range(size)]


def pick(source, rows):
    chosen = (rows[:, None] == jnp.arange(source.shape[0], dtype=jnp.int32)[None, :]).astype(source.dtype)
    return jnp.dot(chosen, source, preferred_element_type=jnp.float32).astype(source.dtype)


def pad_rows(block, count):
    return jnp.pad(block, ((0, count - block.shape[0]), (0, 0)))


def local(integrals, tile_mask, virt_irrep, occ_pairs, virt_energy, occ_energy, amp_ab, amp_cd):
    rows_dev = integrals.shape[0]
    cols_dev = integrals.shape[1]
    nzl, nx, ncore, ny, nzh = (lax.axis_size(a) for a in ("zl", "x", "core", "y", "zh"))
    zl, x, core, y, zh = (lax.axis_index(a) for a in ("zl", "x", "core", "y", "zh"))
    row_group = (zl * nx + x) * ncore + core
    col_group = y * nzh + zh
    nab = rows_dev * nzl * nx * ncore
    cd_count = amp_cd.shape[0]
    ab_count = amp_ab.shape[0]
    y_rows = nzh * ab_count
    y_pad = 40
    x_rows = nzl * cd_count
    x_pad = 40

    other = send(amp_ab, "zh", shift(nzh, 1))

    own = pad_rows(amp_cd, 8)
    own = jnp.concatenate([own, send(own, "zl", [(i, i ^ 1) for i in range(nzl)])], axis=0)
    own = jnp.concatenate([own] + [send(own, "zl", shift(nzl, -s)) for s in (2, 4)], axis=0)

    row_first = row_group * rows_dev
    col_first = nab + col_group * cols_dev
    left, right = window(virt_irrep, row_first, rows_dev)
    row_irrep = jnp.bitwise_xor(left, right)
    left, right = window(virt_irrep, col_first, cols_dev)
    col_irrep = jnp.bitwise_xor(left, right)
    tiles = jnp.repeat(tile_mask, TILE, axis=1)
    col_code = jnp.where(tiles == 1, col_irrep[None, :], -1)
    keep = row_irrep.reshape(-1, TILE)[:, :, None] == col_code[:, None, :]
    blocks = integrals.reshape(-1, TILE, cols_dev)
    masked = jnp.where(keep, blocks, jnp.zeros_like(blocks)).reshape(rows_dev, cols_dev)

    all_cd = lax.all_gather(own, ("x", "core"), axis=0, tiled=True)

    first = jnp.where(zh == 0, amp_ab, other)
    second = jnp.where(zh == 0, other, amp_ab)
    both = pad_rows(jnp.concatenate([first, second], axis=0), y_pad)
    all_ab = lax.all_gather(both, "y", axis=0, tiled=True)

    out = jnp.arange(ny * y_pad, dtype=jnp.int32)
    r = out % y_pad
    to_zh = (zh + 1 + r // ab_count) % nzh
    k = ((out // y_pad) * nzh + to_zh) * ab_count + r % ab_count
    group = k // cd_count
    z = group // (nx * ncore)
    place = (group % (nx * ncore)) * nzl + (z // 2 - zl // 2) % (nzl // 2) * 2 + (z - zl) % 2
    amp = pick(all_cd, jnp.where(r < y_rows, place * 8 + k % cd_count, -1))
    partial_ab = lax.dot_general(amp, masked, (((1,), (1,)), ((), ())), preferred_element_type=jnp.float32)
    partial_ab = partial_ab.reshape(ny, y_pad, rows_dev)

    out = jnp.arange(ncore * nx * x_pad, dtype=jnp.int32)
    r = out % x_pad
    to_x = (out // x_pad) % nx
    to_core = (core + out // (x_pad * nx)) % ncore
    k = ((r // cd_count * nx + to_x) * ncore + to_core) * cd_count + r % cd_count
    amp = pick(all_ab, jnp.where(r < x_rows, k // y_rows * y_pad + k % y_rows, -1))
    partial_cd = jnp.dot(amp, masked, preferred_element_type=jnp.float32)

    total = lax.psum_scatter(partial_ab, "y", scatter_dimension=0, tiled=False)
    ladder_ab = total[ab_count:y_rows] + send(total[:ab_count], "zh", shift(nzh, 1))

    half = nx * x_pad
    total = partial_cd[:half] + send(partial_cd[half:], "core", shift(ncore, 1))
    total = jnp.sum(lax.all_to_all(total.reshape(nx, x_pad, cols_dev), "x", 0, 0), axis=0)
    total = total[:x_rows].reshape(nzl, cd_count, cols_dev)
    ladder_cd = jnp.sum(lax.all_to_all(total, "zl", 0, 0), axis=0)

    places = jnp.concatenate(
        [
            lax.dynamic_slice_in_dim(occ_pairs, col_group * ab_count, ab_count, 1),
            lax.dynamic_slice_in_dim(occ_pairs, row_group * cd_count, cd_count, 1),
        ],
        axis=1,
    )
    equal = places[:, :, None] == jnp.arange(occ_energy.shape[0], dtype=jnp.int32)[None, None, :]
    occ = jnp.sum(jnp.where(equal, occ_energy[None, None, :], 0.0), axis=2)
    occ = occ[0] + occ[1]
    left, right = window(virt_energy, row_first, rows_dev)
    update_ab = ladder_ab / ((left + right)[None, :] - occ[:ab_count, None])
    left, right = window(virt_energy, col_first, cols_dev)
    update_cd = ladder_cd / ((left + right)[None, :] - occ[ab_count:, None])
    return (update_ab, update_cd)


def solution(mesh):
    fine = Mesh(mesh.devices.reshape(6, 4, 2, 8, 2), AB + CD)
    return jax.shard_map(
        local,
        mesh=fine,
        in_specs=(P(AB, CD), P(AB, CD), P(), P(), P(), P(), P(CD, AB), P(AB, CD)),
        out_specs=(P(CD, AB), P(AB, CD)),
        check_vma=False,
    )
```

```python
import jax
import jax.numpy as jnp
from jax import lax
from jax.sharding import Mesh
from jax.sharding import PartitionSpec as P

NV = 1000
TILE = 256
AB = ("zl", "x", "core")
CD = ("y", "zh")


def window(table, first, count):
    spans = (count + NV - 1) // NV + 1
    start = first % NV
    heads = lax.dynamic_slice_in_dim(table, first // NV, spans, 0)
    step = (start + jnp.arange(count, dtype=jnp.int32)) // NV
    left = jnp.where(step == 0, heads[0], heads[spans - 1])
    for j in range(1, spans - 1):
        left = jnp.where(step == j, heads[j], left)
    right = lax.dynamic_slice_in_dim(jnp.concatenate([table] * (spans + 1)), start, count, 0)
    return left, right


def send(block, axis, pairs):
    return lax.ppermute(block, axis, pairs)


def shift(size, by):
    return [(i, (i + by) % size) for i in range(size)]


def gather(block, axis, size):
    return lax.all_to_all(jnp.broadcast_to(block[None], (size,) + block.shape), axis, 0, 0)


def pick(source, rows):
    chosen = (rows[:, None] == jnp.arange(source.shape[0], dtype=jnp.int32)[None, :]).astype(source.dtype)
    return jnp.dot(chosen, source, preferred_element_type=jnp.float32).astype(source.dtype)


def pad_rows(block, count):
    return jnp.pad(block, ((0, count - block.shape[0]), (0, 0)))


def local(integrals, tile_mask, virt_irrep, occ_pairs, virt_energy, occ_energy, amp_ab, amp_cd):
    rows_dev = integrals.shape[0]
    cols_dev = integrals.shape[1]
    nzl, nx, ncore, ny, nzh = (lax.axis_size(a) for a in ("zl", "x", "core", "y", "zh"))
    zl, x, core, y, zh = (lax.axis_index(a) for a in ("zl", "x", "core", "y", "zh"))
    row_group = (zl * nx + x) * ncore + core
    col_group = y * nzh + zh
    nab = rows_dev * nzl * nx * ncore
    cd_count = amp_cd.shape[0]
    ab_count = amp_ab.shape[0]
    y_rows = nzh * ab_count
    y_pad = 40
    x_rows = nzl * cd_count
    x_pad = 40

    other = send(amp_ab, "zh", shift(nzh, 1))

    own = pad_rows(amp_cd, 8)
    own = jnp.concatenate([own, send(own, "zl", [(i, i ^ 1) for i in range(nzl)])], axis=0)
    own = jnp.concatenate([own] + [send(own, "zl", shift(nzl, -s)) for s in (2, 4)], axis=0)

    row_first = row_group * rows_dev
    col_first = nab + col_group * cols_dev
    left, right = window(virt_irrep, row_first, rows_dev)
    row_irrep = jnp.bitwise_xor(left, right)
    left, right = window(virt_irrep, col_first, cols_dev)
    col_irrep = jnp.bitwise_xor(left, right)
    tiles = jnp.repeat(tile_mask, TILE, axis=1)
    col_code = jnp.where(tiles == 1, col_irrep[None, :], -1)
    keep = row_irrep.reshape(-1, TILE)[:, :, None] == col_code[:, None, :]
    blocks = integrals.reshape(-1, TILE, cols_dev)
    masked = jnp.where(keep, blocks, jnp.zeros_like(blocks)).reshape(rows_dev, cols_dev)

    all_cd = lax.all_gather(own, ("x", "core"), axis=0, tiled=True)

    first = jnp.where(zh == 0, amp_ab, other)
    second = jnp.where(zh == 0, other, amp_ab)
    both = pad_rows(jnp.concatenate([first, second], axis=0), y_pad)
    all_ab = gather(both, "y", ny).reshape(ny * y_pad, rows_dev)

    out = jnp.arange(ny * y_pad, dtype=jnp.int32)
    r = out % y_pad
    to_zh = (zh + 1 + r // ab_count) % nzh
    k = ((out // y_pad) * nzh + to_zh) * ab_count + r % ab_count
    group = k // cd_count
    z = group // (nx * ncore)
    place = (group % (nx * ncore)) * nzl + (z // 2 - zl // 2) % (nzl // 2) * 2 + (z - zl) % 2
    amp = pick(all_cd, jnp.where(r < y_rows, place * 8 + k % cd_count, -1))
    partial_ab = lax.dot_general(amp, masked, (((1,), (1,)), ((), ())), preferred_element_type=jnp.float32)
    partial_ab = partial_ab.reshape(ny, y_pad, rows_dev)

    out = jnp.arange(ncore * nx * x_pad, dtype=jnp.int32)
    r = out % x_pad
    to_x = (out // x_pad) % nx
    to_core = (core + out // (x_pad * nx)) % ncore
    k = ((r // cd_count * nx + to_x) * ncore + to_core) * cd_count + r % cd_count
    amp = pick(all_ab, jnp.where(r < x_rows, k // y_rows * y_pad + k % y_rows, -1))
    partial_cd = jnp.dot(amp, masked, preferred_element_type=jnp.float32)

    total_ab = lax.psum_scatter(partial_ab, "y", scatter_dimension=0, tiled=False)

    half = nx * x_pad
    total = partial_cd[:half] + send(partial_cd[half:], "core", shift(ncore, 1))
    total = jnp.sum(lax.all_to_all(total.reshape(nx, x_pad, cols_dev), "x", 0, 0), axis=0)
    total, total_ab = lax.optimization_barrier((total, total_ab))
    ladder_ab = total_ab[ab_count:y_rows] + send(total_ab[:ab_count], "zh", shift(nzh, 1))
    total = total[:x_rows].reshape(nzl, cd_count, cols_dev)
    ladder_cd = jnp.sum(lax.all_to_all(total, "zl", 0, 0), axis=0)

    places = jnp.concatenate(
        [
            lax.dynamic_slice_in_dim(occ_pairs, col_group * ab_count, ab_count, 1),
            lax.dynamic_slice_in_dim(occ_pairs, row_group * cd_count, cd_count, 1),
        ],
        axis=1,
    )
    equal = places[:, :, None] == jnp.arange(occ_energy.shape[0], dtype=jnp.int32)[None, None, :]
    occ = jnp.sum(jnp.where(equal, occ_energy[None, None, :], 0.0), axis=2)
    occ = occ[0] + occ[1]
    left, right = window(virt_energy, row_first, rows_dev)
    update_ab = ladder_ab / ((left + right)[None, :] - occ[:ab_count, None])
    left, right = window(virt_energy, col_first, cols_dev)
    update_cd = ladder_cd / ((left + right)[None, :] - occ[ab_count:, None])
    return (update_ab, update_cd)


def solution(mesh):
    fine = Mesh(mesh.devices.reshape(6, 4, 2, 8, 2), AB + CD)
    return jax.shard_map(
        local,
        mesh=fine,
        in_specs=(P(AB, CD), P(AB, CD), P(), P(), P(), P(), P(CD, AB), P(AB, CD)),
        out_specs=(P(CD, AB), P(AB, CD)),
        check_vma=False,
    )
```

```python
import jax
import jax.numpy as jnp
from jax import lax
from jax.sharding import Mesh
from jax.sharding import PartitionSpec as P

NV = 1000
TILE = 256
AB = ("zl", "x", "core")
CD = ("y", "zh")


def window(table, first, count):
    spans = (count + NV - 1) // NV + 1
    start = first % NV
    heads = lax.dynamic_slice_in_dim(table, first // NV, spans, 0)
    step = (start + jnp.arange(count, dtype=jnp.int32)) // NV
    left = jnp.where(step == 0, heads[0], heads[spans - 1])
    for j in range(1, spans - 1):
        left = jnp.where(step == j, heads[j], left)
    right = lax.dynamic_slice_in_dim(jnp.concatenate([table] * (spans + 1)), start, count, 0)
    return left, right


def send(block, axis, pairs):
    return lax.ppermute(block, axis, pairs)


def shift(size, by):
    return [(i, (i + by) % size) for i in range(size)]


def gather(block, axis, size):
    return lax.all_to_all(jnp.broadcast_to(block[None], (size,) + block.shape), axis, 0, 0)


def pick(source, rows):
    chosen = (rows[:, None] == jnp.arange(source.shape[0], dtype=jnp.int32)[None, :]).astype(source.dtype)
    return jnp.dot(chosen, source, preferred_element_type=jnp.float32).astype(source.dtype)


def encode(sums, rows, axis_rows):
    largest = jnp.max(jnp.abs(sums), axis=1, keepdims=True)
    scale = jnp.ceil(jnp.log2(jnp.maximum(largest, 2.0**-120)) * 256.0)
    parts = jnp.floor(sums * jnp.exp2(scale * (-1.0 / 256.0)) * 32767.0 + 0.5)
    row = lax.broadcasted_iota(jnp.int32, (1, axis_rows, 1), 1)
    return jnp.clip(jnp.where(row == rows, scale, parts), -32767.0, 32767.0).astype(jnp.int16)


def decode_sum(coded, rows):
    scale = jnp.exp2(coded[:, rows : rows + 1].astype(jnp.float32) * (1.0 / 256.0)) * (1.0 / 32767.0)
    return jnp.sum(coded[:, :rows].astype(jnp.float32) * scale, axis=0)


def pad_rows(block, count):
    return jnp.pad(block, ((0, count - block.shape[0]), (0, 0)))


def local(integrals, tile_mask, virt_irrep, occ_pairs, virt_energy, occ_energy, amp_ab, amp_cd):
    rows_dev = integrals.shape[0]
    cols_dev = integrals.shape[1]
    nzl, nx, ncore, ny, nzh = (lax.axis_size(a) for a in ("zl", "x", "core", "y", "zh"))
    zl, x, core, y, zh = (lax.axis_index(a) for a in ("zl", "x", "core", "y", "zh"))
    row_group = (zl * nx + x) * ncore + core
    col_group = y * nzh + zh
    nab = rows_dev * nzl * nx * ncore
    cd_count = amp_cd.shape[0]
    ab_count = amp_ab.shape[0]
    y_rows = nzh * ab_count
    y_pad = 40
    x_rows = nzl * cd_count
    x_pad = 40

    other = send(amp_ab, "zh", shift(nzh, 1))

    own = pad_rows(amp_cd, 8)
    own = jnp.concatenate([own, send(own, "zl", [(i, i ^ 1) for i in range(nzl)])], axis=0)

    row_first = row_group * rows_dev
    col_first = nab + col_group * cols_dev
    left, right = window(virt_irrep, row_first, rows_dev)
    row_irrep = jnp.bitwise_xor(left, right)
    left, right = window(virt_irrep, col_first, cols_dev)
    col_irrep = jnp.bitwise_xor(left, right)
    tiles = jnp.repeat(tile_mask, TILE, axis=1)
    col_code = jnp.where(tiles == 1, col_irrep[None, :], -1)
    own, row_irrep, col_code = lax.optimization_barrier((own, row_irrep, col_code))
    own = jnp.concatenate([own] + [send(own, "zl", shift(nzl, -s)) for s in (2, 4)], axis=0)
    keep = row_irrep.reshape(-1, TILE)[:, :, None] == col_code[:, None, :]
    blocks = integrals.reshape(-1, TILE, cols_dev)
    masked = jnp.where(keep, blocks, jnp.zeros_like(blocks)).reshape(rows_dev, cols_dev)

    all_cd = lax.all_gather(own, ("x", "core"), axis=0, tiled=True)

    first = jnp.where(zh == 0, amp_ab, other)
    second = jnp.where(zh == 0, other, amp_ab)
    both = pad_rows(jnp.concatenate([first, second], axis=0), y_pad)
    all_ab = gather(both, "y", ny).reshape(ny * y_pad, rows_dev)

    out = jnp.arange(ny * y_pad, dtype=jnp.int32)
    r = out % y_pad
    to_zh = (zh + 1 + r // ab_count) % nzh
    k = ((out // y_pad) * nzh + to_zh) * ab_count + r % ab_count
    group = k // cd_count
    z = group // (nx * ncore)
    place = (group % (nx * ncore)) * nzl + (z // 2 - zl // 2) % (nzl // 2) * 2 + (z - zl) % 2
    amp = pick(all_cd, jnp.where(r < y_rows, place * 8 + k % cd_count, -1))
    partial_ab = lax.dot_general(amp, masked, (((1,), (1,)), ((), ())), preferred_element_type=jnp.float32)
    partial_ab = partial_ab.reshape(ny, y_pad, rows_dev)

    out = jnp.arange(ncore * nx * x_pad, dtype=jnp.int32)
    r = out % x_pad
    to_x = (x + out // x_pad) % nx
    to_core = (core + out // (x_pad * nx)) % ncore
    k = ((r // cd_count * nx + to_x) * ncore + to_core) * cd_count + r % cd_count
    amp = pick(all_ab, jnp.where(r < x_rows, k // y_rows * y_pad + k % y_rows, -1))
    partial_cd = jnp.dot(amp, masked, preferred_element_type=jnp.float32)

    coded = encode(partial_ab, y_rows, y_pad)
    coded, virt_energy, occ_pairs = lax.optimization_barrier((coded, virt_energy, occ_pairs))
    coded = lax.all_to_all(coded, "y", 0, 0)

    half = nx * x_pad
    total = partial_cd[:half] + send(partial_cd[half:], "core", shift(ncore, 1))
    total = total.reshape(nx, x_pad, cols_dev)
    near, far, back = (send(total[t], "x", shift(nx, t)) for t in range(1, nx))
    coded, near = lax.optimization_barrier((coded, near))
    total_ab = decode_sum(coded, y_rows)
    ladder_ab = total_ab[ab_count:] + send(total_ab[:ab_count], "zh", shift(nzh, 1))
    total = (total[0] + near) + (far + back)
    total = total[:x_rows].reshape(nzl, cd_count, cols_dev)
    ladder_cd = jnp.sum(lax.all_to_all(total, "zl", 0, 0), axis=0)

    places = jnp.concatenate(
        [
            lax.dynamic_slice_in_dim(occ_pairs, col_group * ab_count, ab_count, 1),
            lax.dynamic_slice_in_dim(occ_pairs, row_group * cd_count, cd_count, 1),
        ],
        axis=1,
    )
    equal = places[:, :, None] == jnp.arange(occ_energy.shape[0], dtype=jnp.int32)[None, None, :]
    occ = jnp.sum(jnp.where(equal, occ_energy[None, None, :], 0.0), axis=2)
    occ = occ[0] + occ[1]
    left, right = window(virt_energy, row_first, rows_dev)
    update_ab = ladder_ab / ((left + right)[None, :] - occ[:ab_count, None])
    left, right = window(virt_energy, col_first, cols_dev)
    update_cd = ladder_cd / ((left + right)[None, :] - occ[ab_count:, None])
    return (update_ab, update_cd)


def solution(mesh):
    fine = Mesh(mesh.devices.reshape(6, 4, 2, 8, 2), AB + CD)
    return jax.shard_map(
        local,
        mesh=fine,
        in_specs=(P(AB, CD), P(AB, CD), P(), P(), P(), P(), P(CD, AB), P(AB, CD)),
        out_specs=(P(CD, AB), P(AB, CD)),
        check_vma=False,
    )
```

```python
import functools

import jax
import jax.numpy as jnp
from jax import lax
from jax.experimental import pallas as pl
from jax.experimental.pallas import tpu as pltpu
from jax.sharding import Mesh
from jax.sharding import PartitionSpec as P

NV = 1000
TILE = 256
LANES = 128
TABLE = 2048
AB = ("zl", "x", "core")
CD = ("y", "zh")
VMEM_LIMIT = 52 * 1024 * 1024
MASK_LIMIT = 60 * 1024 * 1024


def send(block, axis, pairs):
    return lax.ppermute(block, axis, pairs)


def shift(size, by):
    return [(i, (i + by) % size) for i in range(size)]


def gather(block, axis, size):
    return lax.all_to_all(jnp.broadcast_to(block[None], (size,) + block.shape), axis, 0, 0)


def chooser(rows, count):
    return (rows[:, None] == jnp.arange(count, dtype=jnp.int32)[None, :]).astype(jnp.bfloat16)


def pad_rows(block, count):
    return jnp.pad(block, ((0, count - block.shape[0]), (0, 0)))


def masked_kernel(
    place, tile_mask, irrep, energy, pairs, occ, irreps, energies, blocks, masked, den_ab, den_cd, table, row, col
):
    step = pl.program_id(0)
    rows_dev = row.shape[1]
    cols_dev = col.shape[1]

    def window(start, head, count):
        lane = lax.broadcasted_iota(jnp.int32, (1, count), 1)
        labels = jnp.zeros((1, count), jnp.int32)
        sums = jnp.zeros((1, count), jnp.float32)
        for j in range((count + NV - 1) // NV + 1):
            offset = j * NV - start
            turned = pltpu.roll(table[...], (offset + TABLE) % TABLE, 1)[:, :count]
            inside = (lane >= offset) & (lane < offset + NV)
            labels = jnp.where(inside, turned[0:1].astype(jnp.int32) ^ irrep[head + j], labels)
            sums = jnp.where(inside, turned[1:2] + energy[head + j], sums)
        return labels.astype(jnp.float32), sums

    def denominators(out, sums, first):
        for r in range(out.shape[0]):
            out[r : r + 1, :] = sums - (occ[pairs[0, first + r]] + occ[pairs[1, first + r]])

    @pl.when(step == 0)
    def _():
        table[...] = jnp.zeros_like(table)
        table[0:1, :NV] = irreps[...].astype(jnp.float32)
        table[1:2, :NV] = energies[...]
        labels, sums = window(place[0], place[1], rows_dev)
        row[...] = jnp.broadcast_to(labels, row.shape)
        denominators(den_ab, sums, place[4])
        labels, sums = window(place[2], place[3], cols_dev)
        col[...] = jnp.broadcast_to(labels, col.shape)
        denominators(den_cd, sums, place[5])

    across = row[0:1, pl.ds(pl.multiple_of(step * TILE, TILE), TILE)]
    down = jnp.transpose(jnp.broadcast_to(across, (LANES, TILE)))
    for c in range(cols_dev // LANES):
        lanes = slice(c * LANES, (c + 1) * LANES)
        label = jnp.where(tile_mask[step, c * LANES // TILE] == 1, col[0:1, lanes], -1.0)
        block = blocks[:, lanes].astype(jnp.float32)
        masked[:, lanes] = jnp.where(down == label, block, 0.0).astype(masked.dtype)


def ab_kernel(groups, used, choose, amps, masked, coded, chosen):
    @pl.when(pl.program_id(0) == 0)
    def _():
        for c in range(0, amps.shape[1], TILE):
            part = jnp.dot(choose[...], amps[:, c : c + TILE], preferred_element_type=jnp.float32)
            chosen[:, c : c + TILE] = part.astype(chosen.dtype)

    sums = lax.dot_general(
        chosen[...], masked[...], (((1,), (1,)), ((), ())), preferred_element_type=jnp.float32
    )
    rows, columns = sums.shape
    sums = sums.reshape(groups, rows // groups, columns)
    largest = jnp.max(jnp.abs(sums), axis=1, keepdims=True)
    scale = jnp.ceil(jnp.log2(jnp.maximum(largest, 2.0**-120)) * 256.0)
    parts = jnp.floor(sums * jnp.exp2(scale * (-1.0 / 256.0)) * 32767.0 + 0.5)
    place = lax.broadcasted_iota(jnp.int32, sums.shape, 1)
    parts = jnp.clip(jnp.where(place == used, scale, parts), -32767.0, 32767.0)
    coded[...] = parts.reshape(rows, columns).astype(jnp.int32).astype(jnp.int16)


def cd_kernel(choose, amps, masked, keep, give, chosen):
    @pl.when(pl.program_id(0) == 0)
    def _():
        for c in range(0, amps.shape[1], TILE):
            part = jnp.dot(choose[...], amps[:, c : c + TILE], preferred_element_type=jnp.float32)
            chosen[:, c : c + TILE] = part.astype(chosen.dtype)

    sums = jnp.dot(chosen[...], masked[...], preferred_element_type=jnp.float32)
    half = keep.shape[0]
    keep[...] = sums[:half]
    give[...] = sums[half:]


def decode_sum(coded, rows):
    scale = jnp.exp2(coded[:, rows : rows + 1].astype(jnp.float32) * (1.0 / 256.0)) * (1.0 / 32767.0)
    return jnp.sum(coded[:, :rows].astype(jnp.float32) * scale, axis=0)


def local(integrals, tile_mask, virt_irrep, occ_pairs, virt_energy, occ_energy, amp_ab, amp_cd):
    rows_dev = integrals.shape[0]
    cols_dev = integrals.shape[1]
    nzl, nx, ncore, ny, nzh = (lax.axis_size(a) for a in ("zl", "x", "core", "y", "zh"))
    zl, x, core, y, zh = (lax.axis_index(a) for a in ("zl", "x", "core", "y", "zh"))
    row_group = (zl * nx + x) * ncore + core
    col_group = y * nzh + zh
    nab = rows_dev * nzl * nx * ncore
    cd_count = amp_cd.shape[0]
    ab_count = amp_ab.shape[0]
    y_rows = nzh * ab_count
    y_pad = 40
    x_rows = nzl * cd_count
    x_pad = 40
    ab_rows = ny * y_pad
    cd_rows = ncore * nx * x_pad
    params = pltpu.CompilerParams(vmem_limit_bytes=VMEM_LIMIT)

    count = nzl * nx * ncore * 8
    half = cd_rows // ncore

    def ab_chooser():
        out = jnp.arange(ab_rows, dtype=jnp.int32)
        r = out % y_pad
        to_zh = (zh + 1 + r // ab_count) % nzh
        k = ((out // y_pad) * nzh + to_zh) * ab_count + r % ab_count
        group = k // cd_count
        offset = ((group - core) % ncore) * nx + (group // ncore) % nx
        source = (offset * nzl + group // (nx * ncore)) * 8 + k % cd_count
        return chooser(jnp.where(r < y_rows, source, -1), count)

    def cd_chooser():
        out = jnp.arange(cd_rows, dtype=jnp.int32)
        r = out % x_pad
        to_x = (x + out // x_pad) % nx
        to_core = (core + out // (x_pad * nx)) % ncore
        k = ((r // cd_count * nx + to_x) * ncore + to_core) * cd_count + r % cd_count
        return chooser(jnp.where(r < x_rows, k // y_rows * y_pad + k % y_rows, -1), ab_rows)

    other = send(amp_ab, "zh", shift(nzh, 1))
    first = jnp.where(zh == 0, amp_ab, other)
    second = jnp.where(zh == 0, other, amp_ab)
    both = pad_rows(jnp.concatenate([first, second], axis=0), y_pad)

    own = gather(pad_rows(amp_cd, 8), "zl", nzl).reshape(nzl * 8, cols_dev)

    row_first = row_group * rows_dev
    col_first = nab + col_group * cols_dev
    place = jnp.stack(
        [row_first % NV, row_first // NV, col_first % NV, col_first // NV, col_group * ab_count, row_group * cd_count]
    ).astype(jnp.int32)
    smem = pl.BlockSpec(memory_space=pltpu.SMEM)
    masked, den_ab, den_cd = pl.pallas_call(
        masked_kernel,
        grid=(rows_dev // TILE,),
        in_specs=[smem] * 6
        + [
            pl.BlockSpec((1, NV), lambda i: (0, 0)),
            pl.BlockSpec((1, NV), lambda i: (0, 0)),
            pl.BlockSpec((TILE, cols_dev), lambda i: (i, 0)),
        ],
        out_specs=[
            pl.BlockSpec((TILE, cols_dev), lambda i: (i, 0)),
            pl.BlockSpec((ab_count, rows_dev), lambda i: (0, 0)),
            pl.BlockSpec((cd_count, cols_dev), lambda i: (0, 0)),
        ],
        out_shape=[
            jax.ShapeDtypeStruct(integrals.shape, integrals.dtype),
            jax.ShapeDtypeStruct((ab_count, rows_dev), jnp.float32),
            jax.ShapeDtypeStruct((cd_count, cols_dev), jnp.float32),
        ],
        scratch_shapes=[
            pltpu.VMEM((8, TABLE), jnp.float32),
            pltpu.VMEM((8, rows_dev), jnp.float32),
            pltpu.VMEM((8, cols_dev), jnp.float32),
        ],
        compiler_params=pltpu.CompilerParams(vmem_limit_bytes=MASK_LIMIT),
        cost_estimate=pl.CostEstimate(flops=4 * rows_dev * cols_dev, bytes_accessed=4 * rows_dev * cols_dev, transcendentals=0),
        name="masked",
    )(
        place,
        tile_mask,
        virt_irrep,
        virt_energy,
        occ_pairs,
        occ_energy,
        virt_irrep.reshape(1, NV),
        virt_energy.reshape(1, NV),
        integrals,
    )

    choose_ab, choose_cd = ab_chooser(), cd_chooser()
    own, masked, both, choose_ab, choose_cd = lax.optimization_barrier((own, masked, both, choose_ab, choose_cd))
    own = lax.all_gather(own, "x", axis=0, tiled=True)
    all_cd = jnp.concatenate([own, send(own, "core", shift(ncore, 1))], axis=0)
    all_ab = gather(both, "y", ny).reshape(ab_rows, rows_dev)

    coded = pl.pallas_call(
        functools.partial(ab_kernel, ny, y_rows),
        grid=(rows_dev // TILE,),
        in_specs=[
            pl.BlockSpec((ab_rows, count), lambda i: (0, 0)),
            pl.BlockSpec((count, cols_dev), lambda i: (0, 0)),
            pl.BlockSpec((TILE, cols_dev), lambda i: (i, 0)),
        ],
        out_specs=pl.BlockSpec((ab_rows, TILE), lambda i: (0, i)),
        out_shape=jax.ShapeDtypeStruct((ab_rows, rows_dev), jnp.int16),
        scratch_shapes=[pltpu.VMEM((ab_rows, cols_dev), jnp.bfloat16)],
        compiler_params=params,
        cost_estimate=pl.CostEstimate(
            flops=2 * ab_rows * cols_dev * (rows_dev + count), bytes_accessed=2 * rows_dev * cols_dev, transcendentals=0
        ),
        name="ab_product",
    )(choose_ab, all_cd, masked)

    all_ab, coded = lax.optimization_barrier((all_ab, coded))
    keep, give = pl.pallas_call(
        cd_kernel,
        grid=(cols_dev // TILE,),
        in_specs=[
            pl.BlockSpec((cd_rows, ab_rows), lambda i: (0, 0)),
            pl.BlockSpec((ab_rows, rows_dev), lambda i: (0, 0)),
            pl.BlockSpec((rows_dev, TILE), lambda i: (0, i)),
        ],
        out_specs=[pl.BlockSpec((half, TILE), lambda i: (0, i))] * 2,
        out_shape=[jax.ShapeDtypeStruct((half, cols_dev), jnp.float32)] * 2,
        scratch_shapes=[pltpu.VMEM((cd_rows, rows_dev), jnp.bfloat16)],
        compiler_params=params,
        cost_estimate=pl.CostEstimate(
            flops=2 * cd_rows * rows_dev * (cols_dev + ab_rows), bytes_accessed=2 * rows_dev * cols_dev, transcendentals=0
        ),
        name="cd_product",
    )(choose_cd, all_ab, masked)

    coded = lax.all_to_all(coded.reshape(ny, y_pad, rows_dev), "y", 0, 0)

    total = keep + send(give, "core", shift(ncore, 1))
    total = total.reshape(nx, x_pad, cols_dev)
    near, far, back = (send(total[t], "x", shift(nx, t)) for t in range(1, nx))
    coded, near = lax.optimization_barrier((coded, near))
    total_ab = decode_sum(coded, y_rows)
    ladder_ab = total_ab[ab_count:] + send(total_ab[:ab_count], "zh", shift(nzh, 1))
    total = (total[0] + near) + (far + back)
    total = total[:x_rows].reshape(nzl, cd_count, cols_dev)
    ladder_cd = jnp.sum(lax.all_to_all(total, "zl", 0, 0), axis=0)
    return (ladder_ab / den_ab, ladder_cd / den_cd)


def solution(mesh):
    fine = Mesh(mesh.devices.reshape(6, 4, 2, 8, 2), AB + CD)
    return jax.shard_map(
        local,
        mesh=fine,
        in_specs=(P(AB, CD), P(AB, CD), P(), P(), P(), P(), P(CD, AB), P(AB, CD)),
        out_specs=(P(CD, AB), P(AB, CD)),
        check_vma=False,
    )
```

```python
import functools

import jax
import jax.numpy as jnp
from jax import lax
from jax.experimental import pallas as pl
from jax.experimental.pallas import tpu as pltpu
from jax.sharding import Mesh
from jax.sharding import PartitionSpec as P

NV = 1000
TILE = 256
LANES = 128
TABLE = 2048
AB = ("zl", "x", "core")
CD = ("y", "zh")
VMEM_LIMIT = 52 * 1024 * 1024
MASK_LIMIT = 60 * 1024 * 1024


def send(block, axis, pairs):
    return lax.ppermute(block, axis, pairs)


def shift(size, by):
    return [(i, (i + by) % size) for i in range(size)]


def copied(block, size):
    return jnp.broadcast_to(block[None], (size,) + block.shape)


def chooser(rows, count):
    return (rows[:, None] == jnp.arange(count, dtype=jnp.int32)[None, :]).astype(jnp.bfloat16)


def pad_rows(block, count):
    return jnp.pad(block, ((0, count - block.shape[0]), (0, 0)))


def copies(masked, held, arrived, axis):
    parts = []
    for j in range(masked.shape[axis] // TILE):
        span = pl.ds(j * TILE, TILE)
        at = (span, slice(None)) if axis == 0 else (slice(None), span)
        parts.append(pltpu.make_async_copy(masked.at[at], held.at[at], arrived.at[j]))
        parts[-1].start()
    return parts


def masked_kernel(
    place, tile_mask, irrep, energy, pairs, occ, irreps, energies, blocks, masked, den_ab, den_cd,
    table, held, kept, arrived, stored
):
    rows_dev = den_ab.shape[1]
    cols_dev = den_cd.shape[1]
    parts = copies(blocks, held, arrived, 0)

    def window(start, head, count):
        lane = lax.broadcasted_iota(jnp.int32, (1, count), 1)
        labels = jnp.zeros((1, count), jnp.int32)
        sums = jnp.zeros((1, count), jnp.float32)
        for j in range((count + NV - 1) // NV + 1):
            offset = j * NV - start
            turned = pltpu.roll(table[...], (offset + TABLE) % TABLE, 1)[:, :count]
            inside = (lane >= offset) & (lane < offset + NV)
            labels = jnp.where(inside, turned[0:1].astype(jnp.int32) ^ irrep[head + j], labels)
            sums = jnp.where(inside, turned[1:2] + energy[head + j], sums)
        return labels.astype(jnp.float32), sums

    def denominators(out, sums, first):
        for r in range(out.shape[0]):
            out[r : r + 1, :] = sums - (occ[pairs[0, first + r]] + occ[pairs[1, first + r]])

    table[...] = jnp.zeros_like(table)
    table[0:1, :NV] = irreps[...].astype(jnp.float32)
    table[1:2, :NV] = energies[...]
    row, sums = window(place[0], place[1], rows_dev)
    denominators(den_ab, sums, place[4])
    col, sums = window(place[2], place[3], cols_dev)
    denominators(den_cd, sums, place[5])
    leaving = []
    for j, part in enumerate(parts):
        span = slice(j * TILE, (j + 1) * TILE)
        down = jnp.transpose(jnp.broadcast_to(row[:, span], (LANES, TILE)))
        part.wait()
        for c in range(cols_dev // LANES):
            lanes = slice(c * LANES, (c + 1) * LANES)
            label = jnp.where(tile_mask[j, c * LANES // TILE] == 1, col[:, lanes], -1.0)
            block = held[span, lanes].astype(jnp.float32)
            kept[span, lanes] = jnp.where(down == label, block, 0.0).astype(kept.dtype)
        leaving.append(pltpu.make_async_copy(kept.at[span, :], masked.at[span, :], stored.at[j]))
        leaving[-1].start()
    for part in leaving:
        part.wait()


def ab_kernel(groups, used, choose, amps, masked, coded, chosen):
    @pl.when(pl.program_id(0) == 0)
    def _():
        for c in range(0, amps.shape[1], TILE):
            part = jnp.dot(choose[...], amps[:, c : c + TILE], preferred_element_type=jnp.float32)
            chosen[:, c : c + TILE] = part.astype(chosen.dtype)

    sums = lax.dot_general(
        chosen[...], masked[...], (((1,), (1,)), ((), ())), preferred_element_type=jnp.float32
    )
    rows, columns = sums.shape
    sums = sums.reshape(groups, rows // groups, columns)
    largest = jnp.max(jnp.abs(sums), axis=1, keepdims=True)
    scale = jnp.ceil(jnp.log2(jnp.maximum(largest, 2.0**-120)) * 256.0)
    parts = jnp.floor(sums * jnp.exp2(scale * (-1.0 / 256.0)) * 32767.0 + 0.5)
    place = lax.broadcasted_iota(jnp.int32, sums.shape, 1)
    parts = jnp.clip(jnp.where(place == used, scale, parts), -32767.0, 32767.0)
    coded[...] = parts.reshape(rows, columns).astype(jnp.int32).astype(jnp.int16)


def cd_kernel(choose, amps, masked, keep, give, chosen):
    @pl.when(pl.program_id(0) == 0)
    def _():
        for c in range(0, amps.shape[1], TILE):
            part = jnp.dot(choose[...], amps[:, c : c + TILE], preferred_element_type=jnp.float32)
            chosen[:, c : c + TILE] = part.astype(chosen.dtype)

    sums = jnp.dot(chosen[...], masked[...], preferred_element_type=jnp.float32)
    half = keep.shape[0]
    keep[...] = sums[:half]
    give[...] = sums[half:]


def decode_sum(coded, rows):
    scale = jnp.exp2(coded[:, rows : rows + 1].astype(jnp.float32) * (1.0 / 256.0)) * (1.0 / 32767.0)
    return jnp.sum(coded[:, :rows].astype(jnp.float32) * scale, axis=0)


def local(integrals, tile_mask, virt_irrep, occ_pairs, virt_energy, occ_energy, amp_ab, amp_cd):
    rows_dev = integrals.shape[0]
    cols_dev = integrals.shape[1]
    nzl, nx, ncore, ny, nzh = (lax.axis_size(a) for a in ("zl", "x", "core", "y", "zh"))
    zl, x, core, y, zh = (lax.axis_index(a) for a in ("zl", "x", "core", "y", "zh"))
    row_group = (zl * nx + x) * ncore + core
    col_group = y * nzh + zh
    nab = rows_dev * nzl * nx * ncore
    cd_count = amp_cd.shape[0]
    ab_count = amp_ab.shape[0]
    y_rows = nzh * ab_count
    y_pad = 40
    x_rows = nzl * cd_count
    x_pad = 40
    ab_rows = ny * y_pad
    cd_rows = ncore * nx * x_pad
    params = pltpu.CompilerParams(vmem_limit_bytes=VMEM_LIMIT)

    count = nzl * nx * ncore * 8
    half = cd_rows // ncore

    def ab_chooser():
        out = jnp.arange(ab_rows, dtype=jnp.int32)
        r = out % y_pad
        to_zh = (zh + 1 + r // ab_count) % nzh
        k = ((out // y_pad) * nzh + to_zh) * ab_count + r % ab_count
        group = k // cd_count
        source = ((group % (nx * ncore)) * nzl + group // (nx * ncore)) * 8 + k % cd_count
        return chooser(jnp.where(r < y_rows, source, -1), count)

    def cd_chooser():
        out = jnp.arange(cd_rows, dtype=jnp.int32)
        r = out % x_pad
        to_x = (x + out // x_pad) % nx
        to_core = (core + out // (x_pad * nx)) % ncore
        k = ((r // cd_count * nx + to_x) * ncore + to_core) * cd_count + r % cd_count
        return chooser(jnp.where(r < x_rows, k // y_rows * y_pad + k % y_rows, -1), ab_rows)

    other = send(amp_ab, "zh", shift(nzh, 1))
    first = jnp.where(zh == 0, amp_ab, other)
    second = jnp.where(zh == 0, other, amp_ab)
    both = copied(pad_rows(jnp.concatenate([first, second], axis=0), y_pad), ny)

    own = jnp.pad(copied(amp_cd, nzl), ((0, 0), (0, 8 - cd_count), (0, 0)))
    own = lax.all_to_all(own, "zl", 0, 0).reshape(nzl * 8, cols_dev)

    row_first = row_group * rows_dev
    col_first = nab + col_group * cols_dev
    place = jnp.stack(
        [row_first % NV, row_first // NV, col_first % NV, col_first // NV, col_group * ab_count, row_group * cd_count]
    ).astype(jnp.int32)
    smem = pl.BlockSpec(memory_space=pltpu.SMEM)
    vmem = pl.BlockSpec(memory_space=pltpu.VMEM)
    masked, den_ab, den_cd = pl.pallas_call(
        masked_kernel,
        in_specs=[smem] * 6 + [vmem, vmem, pl.BlockSpec(memory_space=pl.ANY)],
        out_specs=[pl.BlockSpec(memory_space=pl.ANY), vmem, vmem],
        out_shape=[
            jax.ShapeDtypeStruct(integrals.shape, integrals.dtype),
            jax.ShapeDtypeStruct((ab_count, rows_dev), jnp.float32),
            jax.ShapeDtypeStruct((cd_count, cols_dev), jnp.float32),
        ],
        scratch_shapes=[
            pltpu.VMEM((8, TABLE), jnp.float32),
            pltpu.VMEM(integrals.shape, integrals.dtype),
            pltpu.VMEM(integrals.shape, integrals.dtype),
            pltpu.SemaphoreType.DMA((rows_dev // TILE,)),
            pltpu.SemaphoreType.DMA((rows_dev // TILE,)),
        ],
        compiler_params=pltpu.CompilerParams(vmem_limit_bytes=MASK_LIMIT),
        cost_estimate=pl.CostEstimate(flops=4 * rows_dev * cols_dev, bytes_accessed=4 * rows_dev * cols_dev, transcendentals=0),
        name="masked",
    )(
        place,
        tile_mask,
        virt_irrep,
        virt_energy,
        occ_pairs,
        occ_energy,
        virt_irrep.reshape(1, NV),
        virt_energy.reshape(1, NV),
        integrals,
    )

    choose_ab, choose_cd = ab_chooser(), cd_chooser()
    own, masked, both, choose_ab, choose_cd = lax.optimization_barrier((own, masked, both, choose_ab, choose_cd))
    all_cd = lax.all_gather(own, ("x", "core"), axis=0, tiled=True)
    all_ab = lax.all_to_all(both, "y", 0, 0).reshape(ab_rows, rows_dev)

    coded = pl.pallas_call(
        functools.partial(ab_kernel, ny, y_rows),
        grid=(rows_dev // TILE,),
        in_specs=[
            pl.BlockSpec((ab_rows, count), lambda i: (0, 0)),
            pl.BlockSpec((count, cols_dev), lambda i: (0, 0)),
            pl.BlockSpec((TILE, cols_dev), lambda i: (i, 0)),
        ],
        out_specs=pl.BlockSpec((ab_rows, TILE), lambda i: (0, i)),
        out_shape=jax.ShapeDtypeStruct((ab_rows, rows_dev), jnp.int16),
        scratch_shapes=[pltpu.VMEM((ab_rows, cols_dev), jnp.bfloat16)],
        compiler_params=params,
        cost_estimate=pl.CostEstimate(
            flops=2 * ab_rows * cols_dev * (rows_dev + count), bytes_accessed=2 * rows_dev * cols_dev, transcendentals=0
        ),
        name="ab_product",
    )(choose_ab, all_cd, masked)

    all_ab, coded = lax.optimization_barrier((all_ab, coded))
    keep, give = pl.pallas_call(
        cd_kernel,
        grid=(cols_dev // TILE,),
        in_specs=[
            pl.BlockSpec((cd_rows, ab_rows), lambda i: (0, 0)),
            pl.BlockSpec((ab_rows, rows_dev), lambda i: (0, 0)),
            pl.BlockSpec((rows_dev, TILE), lambda i: (0, i)),
        ],
        out_specs=[pl.BlockSpec((half, TILE), lambda i: (0, i))] * 2,
        out_shape=[jax.ShapeDtypeStruct((half, cols_dev), jnp.float32)] * 2,
        scratch_shapes=[pltpu.VMEM((cd_rows, rows_dev), jnp.bfloat16)],
        compiler_params=params,
        cost_estimate=pl.CostEstimate(
            flops=2 * cd_rows * rows_dev * (cols_dev + ab_rows), bytes_accessed=2 * rows_dev * cols_dev, transcendentals=0
        ),
        name="cd_product",
    )(choose_cd, all_ab, masked)

    coded = lax.all_to_all(coded.reshape(ny, y_pad, rows_dev), "y", 0, 0)

    total = keep + send(give, "core", shift(ncore, 1))
    total = total.reshape(nx, x_pad, cols_dev)
    near, far, back = (send(total[t], "x", shift(nx, t)) for t in range(1, nx))
    coded, near = lax.optimization_barrier((coded, near))
    total_ab = decode_sum(coded, y_rows)
    ladder_ab = total_ab[ab_count:] + send(total_ab[:ab_count], "zh", shift(nzh, 1))
    total = (total[0] + near) + (far + back)
    total = total[:x_rows].reshape(nzl, cd_count, cols_dev)
    ladder_cd = jnp.sum(lax.all_to_all(total, "zl", 0, 0), axis=0)
    return (ladder_ab / den_ab, ladder_cd / den_cd)


def solution(mesh):
    fine = Mesh(mesh.devices.reshape(6, 4, 2, 8, 2), AB + CD)
    return jax.shard_map(
        local,
        mesh=fine,
        in_specs=(P(AB, CD), P(AB, CD), P(), P(), P(), P(), P(CD, AB), P(AB, CD)),
        out_specs=(P(CD, AB), P(AB, CD)),
        check_vma=False,
    )
```

```python
import functools

import jax
import jax.numpy as jnp
from jax import lax
from jax.experimental import pallas as pl
from jax.experimental.pallas import tpu as pltpu
from jax.sharding import Mesh
from jax.sharding import PartitionSpec as P

NV = 1000
TILE = 256
LANES = 128
TABLE = 2048
AB = ("zl", "x", "core")
CD = ("y", "zh")
VMEM_LIMIT = 50 * 1024 * 1024
MASK_LIMIT = 60 * 1024 * 1024


def send(block, axis, pairs):
    return lax.ppermute(block, axis, pairs)


def shift(size, by):
    return [(i, (i + by) % size) for i in range(size)]


def copied(block, size):
    return jnp.broadcast_to(block[None], (size,) + block.shape)


def chooser(rows, count):
    return (rows[:, None] == jnp.arange(count, dtype=jnp.int32)[None, :]).astype(jnp.bfloat16)


def pad_rows(block, count):
    return jnp.pad(block, ((0, count - block.shape[0]), (0, 0)))


def copies(masked, held, arrived, axis):
    parts = []
    for j in range(masked.shape[axis] // TILE):
        span = pl.ds(j * TILE, TILE)
        at = (span, slice(None)) if axis == 0 else (slice(None), span)
        parts.append(pltpu.make_async_copy(masked.at[at], held.at[at], arrived.at[j]))
        parts[-1].start()
    return parts


def masked_kernel(
    place, tile_mask, irrep, energy, pairs, occ, irreps, energies, blocks, masked, den_ab, den_cd,
    table, held, kept, arrived, stored
):
    rows_dev = den_ab.shape[1]
    cols_dev = den_cd.shape[1]
    parts = copies(blocks, held, arrived, 0)

    def window(start, head, count):
        lane = lax.broadcasted_iota(jnp.int32, (1, count), 1)
        labels = jnp.zeros((1, count), jnp.int32)
        sums = jnp.zeros((1, count), jnp.float32)
        for j in range((count + NV - 1) // NV + 1):
            offset = j * NV - start
            turned = pltpu.roll(table[...], (offset + TABLE) % TABLE, 1)[:, :count]
            inside = (lane >= offset) & (lane < offset + NV)
            labels = jnp.where(inside, turned[0:1].astype(jnp.int32) ^ irrep[head + j], labels)
            sums = jnp.where(inside, turned[1:2] + energy[head + j], sums)
        return labels.astype(jnp.float32), sums

    def denominators(out, sums, first):
        for r in range(out.shape[0]):
            out[r : r + 1, :] = sums - (occ[pairs[0, first + r]] + occ[pairs[1, first + r]])

    table[...] = jnp.zeros_like(table)
    table[0:1, :NV] = irreps[...].astype(jnp.float32)
    table[1:2, :NV] = energies[...]
    row, sums = window(place[0], place[1], rows_dev)
    denominators(den_ab, sums, place[4])
    col, sums = window(place[2], place[3], cols_dev)
    denominators(den_cd, sums, place[5])
    leaving = []
    for j, part in enumerate(parts):
        span = slice(j * TILE, (j + 1) * TILE)
        down = jnp.transpose(jnp.broadcast_to(row[:, span], (LANES, TILE)))
        part.wait()
        for c in range(cols_dev // LANES):
            lanes = slice(c * LANES, (c + 1) * LANES)
            label = jnp.where(tile_mask[j, c * LANES // TILE] == 1, col[:, lanes], -1.0)
            block = held[span, lanes].astype(jnp.float32)
            kept[span, lanes] = jnp.where(down == label, block, 0.0).astype(kept.dtype)
        leaving.append(pltpu.make_async_copy(kept.at[span, :], masked.at[span, :], stored.at[j]))
        leaving[-1].start()
    for part in leaving:
        part.wait()


def pick(choose, amps, chosen):
    for c in range(0, amps.shape[1], TILE):
        part = jnp.dot(choose[...], amps[:, c : c + TILE], preferred_element_type=jnp.float32)
        chosen[:, c : c + TILE] = part.astype(chosen.dtype)


def ab_kernel(groups, used, choose, amps, masked, coded, chosen, held, arrived):
    parts = copies(masked, held, arrived, 0)
    pick(choose, amps, chosen)
    for j, part in enumerate(parts):
        part.wait()
        span = slice(j * TILE, (j + 1) * TILE)
        sums = lax.dot_general(
            chosen[...], held[span, :], (((1,), (1,)), ((), ())), preferred_element_type=jnp.float32
        )
        rows, columns = sums.shape
        sums = sums.reshape(groups, rows // groups, columns)
        largest = jnp.max(jnp.abs(sums), axis=1, keepdims=True)
        scale = jnp.ceil(jnp.log2(jnp.maximum(largest, 2.0**-120)) * 256.0)
        whole = jnp.floor(sums * jnp.exp2(scale * (-1.0 / 256.0)) * 32767.0 + 0.5)
        place = lax.broadcasted_iota(jnp.int32, sums.shape, 1)
        whole = jnp.clip(jnp.where(place == used, scale, whole), -32767.0, 32767.0)
        coded[:, span] = whole.reshape(rows, columns).astype(jnp.int32).astype(jnp.int16)


def cd_kernel(choose, amps, masked, keep, give, chosen):
    rows, side = chosen.shape[0], amps.shape[1]

    @pl.when(pl.program_id(0) == 0)
    def _():
        for c in range(0, side, TILE):
            part = jnp.dot(choose[...], amps[:, c : c + TILE], preferred_element_type=jnp.float32)
            chosen[:, c : c + TILE] = part[:rows].astype(chosen.dtype)
            chosen[:, side + c : side + c + TILE] = part[rows:].astype(chosen.dtype)

    sums = jnp.dot(chosen[...], masked[...], preferred_element_type=jnp.float32)
    half = keep.shape[0]
    keep[...] = sums[:half]
    give[...] = sums[half:]


def decode_sum(coded, rows):
    scale = jnp.exp2(coded[:, rows : rows + 1].astype(jnp.float32) * (1.0 / 256.0)) * (1.0 / 32767.0)
    return jnp.sum(coded[:, :rows].astype(jnp.float32) * scale, axis=0)


def local(integrals, tile_mask, virt_irrep, occ_pairs, virt_energy, occ_energy, amp_ab, amp_cd):
    rows_dev = integrals.shape[0]
    cols_dev = integrals.shape[1]
    nzl, nx, ncore, ny, nzh = (lax.axis_size(a) for a in ("zl", "x", "core", "y", "zh"))
    zl, x, core, y, zh = (lax.axis_index(a) for a in ("zl", "x", "core", "y", "zh"))
    row_group = (zl * nx + x) * ncore + core
    col_group = y * nzh + zh
    nab = rows_dev * nzl * nx * ncore
    cd_count = amp_cd.shape[0]
    ab_count = amp_ab.shape[0]
    y_rows = nzh * ab_count
    y_pad = 40
    x_rows = nzl * cd_count
    x_pad = 40
    ab_rows = ny * y_pad
    cd_rows = ncore * nx * x_pad
    params = pltpu.CompilerParams(vmem_limit_bytes=VMEM_LIMIT)

    count = nzl * nx * ncore * 8
    half = cd_rows // ncore

    def ab_chooser():
        out = jnp.arange(ab_rows, dtype=jnp.int32)
        r = out % y_pad
        to_zh = (zh + 1 + r // ab_count) % nzh
        k = ((out // y_pad) * nzh + to_zh) * ab_count + r % ab_count
        group = k // cd_count
        source = ((group % (nx * ncore)) * nzl + group // (nx * ncore)) * 8 + k % cd_count
        return chooser(jnp.where(r < y_rows, source, -1), count)

    def cd_chooser():
        out = jnp.arange(cd_rows, dtype=jnp.int32)
        r = out % x_pad
        to_x = (x + out // x_pad) % nx
        to_core = (core + out // (x_pad * nx)) % ncore
        k = ((r // cd_count * nx + to_x) * ncore + to_core) * cd_count + r % cd_count
        source = k // y_rows * 2 * y_rows + k % y_rows
        source = jnp.concatenate([jnp.where(r < x_rows, source + part, -1) for part in (0, y_rows)])
        return chooser(source, 2 * ny * y_rows)

    other = send(amp_ab, "zh", shift(nzh, 1))
    first = jnp.where(zh == 0, amp_ab, other)
    second = jnp.where(zh == 0, other, amp_ab)
    side = rows_dev // 2
    both = jnp.concatenate([first[:, :side], second[:, :side], first[:, side:], second[:, side:]], axis=0)
    both = copied(both, ny)

    own = jnp.pad(copied(amp_cd, nzl), ((0, 0), (0, 8 - cd_count), (0, 0)))
    own = lax.all_to_all(own, "zl", 0, 0).reshape(nzl * 8, cols_dev)

    row_first = row_group * rows_dev
    col_first = nab + col_group * cols_dev
    place = jnp.stack(
        [row_first % NV, row_first // NV, col_first % NV, col_first // NV, col_group * ab_count, row_group * cd_count]
    ).astype(jnp.int32)
    smem = pl.BlockSpec(memory_space=pltpu.SMEM)
    vmem = pl.BlockSpec(memory_space=pltpu.VMEM)
    masked, den_ab, den_cd = pl.pallas_call(
        masked_kernel,
        in_specs=[smem] * 6 + [vmem, vmem, pl.BlockSpec(memory_space=pl.ANY)],
        out_specs=[pl.BlockSpec(memory_space=pl.ANY), vmem, vmem],
        out_shape=[
            jax.ShapeDtypeStruct(integrals.shape, integrals.dtype),
            jax.ShapeDtypeStruct((ab_count, rows_dev), jnp.float32),
            jax.ShapeDtypeStruct((cd_count, cols_dev), jnp.float32),
        ],
        scratch_shapes=[
            pltpu.VMEM((8, TABLE), jnp.float32),
            pltpu.VMEM(integrals.shape, integrals.dtype),
            pltpu.VMEM(integrals.shape, integrals.dtype),
            pltpu.SemaphoreType.DMA((rows_dev // TILE,)),
            pltpu.SemaphoreType.DMA((rows_dev // TILE,)),
        ],
        compiler_params=pltpu.CompilerParams(vmem_limit_bytes=MASK_LIMIT),
        cost_estimate=pl.CostEstimate(flops=4 * rows_dev * cols_dev, bytes_accessed=4 * rows_dev * cols_dev, transcendentals=0),
        name="masked",
    )(
        place,
        tile_mask,
        virt_irrep,
        virt_energy,
        occ_pairs,
        occ_energy,
        virt_irrep.reshape(1, NV),
        virt_energy.reshape(1, NV),
        integrals,
    )

    choose_ab, choose_cd = ab_chooser(), cd_chooser()
    own, masked, both, choose_ab, choose_cd = lax.optimization_barrier((own, masked, both, choose_ab, choose_cd))
    all_cd = lax.all_gather(own, ("x", "core"), axis=0, tiled=True)
    all_ab = lax.all_to_all(both, "y", 0, 0).reshape(2 * ny * y_rows, side)

    coded = pl.pallas_call(
        functools.partial(ab_kernel, ny, y_rows),
        in_specs=[vmem, vmem, pl.BlockSpec(memory_space=pl.ANY)],
        out_specs=vmem,
        out_shape=jax.ShapeDtypeStruct((ab_rows, rows_dev), jnp.int16),
        scratch_shapes=[
            pltpu.VMEM((ab_rows, cols_dev), jnp.bfloat16),
            pltpu.VMEM((rows_dev, cols_dev), jnp.bfloat16),
            pltpu.SemaphoreType.DMA((rows_dev // TILE,)),
        ],
        compiler_params=params,
        cost_estimate=pl.CostEstimate(
            flops=2 * ab_rows * cols_dev * (rows_dev + count), bytes_accessed=2 * rows_dev * cols_dev, transcendentals=0
        ),
        name="ab_product",
    )(choose_ab, all_cd, masked)

    all_ab, coded = lax.optimization_barrier((all_ab, coded))
    keep, give = pl.pallas_call(
        cd_kernel,
        grid=(cols_dev // TILE,),
        in_specs=[
            pl.BlockSpec((2 * cd_rows, 2 * ny * y_rows), lambda i: (0, 0)),
            pl.BlockSpec((2 * ny * y_rows, side), lambda i: (0, 0)),
            pl.BlockSpec((rows_dev, TILE), lambda i: (0, i)),
        ],
        out_specs=[pl.BlockSpec((half, TILE), lambda i: (0, i))] * 2,
        out_shape=[jax.ShapeDtypeStruct((half, cols_dev), jnp.float32)] * 2,
        scratch_shapes=[pltpu.VMEM((cd_rows, rows_dev), jnp.bfloat16)],
        compiler_params=params,
        cost_estimate=pl.CostEstimate(
            flops=2 * cd_rows * rows_dev * (cols_dev + ab_rows), bytes_accessed=2 * rows_dev * cols_dev, transcendentals=0
        ),
        name="cd_product",
    )(choose_cd, all_ab, masked)

    coded = lax.all_to_all(coded.reshape(ny, y_pad, rows_dev), "y", 0, 0)

    total = keep + send(give, "core", shift(ncore, 1))
    total = total.reshape(nx, x_pad, cols_dev)
    near, far, back = (send(total[t], "x", shift(nx, t)) for t in range(1, nx))
    coded, near = lax.optimization_barrier((coded, near))
    total_ab = decode_sum(coded, y_rows)
    ladder_ab = total_ab[ab_count:] + send(total_ab[:ab_count], "zh", shift(nzh, 1))
    total = (total[0] + near) + (far + back)
    total = total[:x_rows].reshape(nzl, cd_count, cols_dev)
    ladder_cd = jnp.sum(lax.all_to_all(total, "zl", 0, 0), axis=0)
    return (ladder_ab / den_ab, ladder_cd / den_cd)


def solution(mesh):
    fine = Mesh(mesh.devices.reshape(6, 4, 2, 8, 2), AB + CD)
    return jax.shard_map(
        local,
        mesh=fine,
        in_specs=(P(AB, CD), P(AB, CD), P(), P(), P(), P(), P(CD, AB), P(AB, CD)),
        out_specs=(P(CD, AB), P(AB, CD)),
        check_vma=False,
    )
```

```python
import functools

import jax
import jax.numpy as jnp
from jax import lax
from jax.experimental import pallas as pl
from jax.experimental.pallas import tpu as pltpu
from jax.sharding import Mesh
from jax.sharding import PartitionSpec as P

NV = 1000
TILE = 256
LANES = 128
TABLE = 2048
AB = ("zl", "x", "core")
CD = ("y", "zh")
VMEM_LIMIT = 50 * 1024 * 1024
MASK_LIMIT = 60 * 1024 * 1024


def send(block, axis, pairs):
    return lax.ppermute(block, axis, pairs)


def shift(size, by):
    return [(i, (i + by) % size) for i in range(size)]


def copied(block, size):
    return jnp.broadcast_to(block[None], (size,) + block.shape)


def chooser(rows, count):
    return (rows[:, None] == jnp.arange(count, dtype=jnp.int32)[None, :]).astype(jnp.bfloat16)


def pad_rows(block, count):
    return jnp.pad(block, ((0, count - block.shape[0]), (0, 0)))


def copies(masked, held, arrived, axis):
    parts = []
    for j in range(masked.shape[axis] // TILE):
        span = pl.ds(j * TILE, TILE)
        at = (span, slice(None)) if axis == 0 else (slice(None), span)
        parts.append(pltpu.make_async_copy(masked.at[at], held.at[at], arrived.at[j]))
        parts[-1].start()
    return parts


def masked_kernel(
    place, tile_mask, irrep, energy, pairs, occ, irreps, energies, blocks, masked, den_ab, den_cd,
    table, held, kept, arrived, stored
):
    rows_dev = den_ab.shape[1]
    cols_dev = den_cd.shape[1]
    parts = copies(blocks, held, arrived, 0)

    def window(start, head, count):
        lane = lax.broadcasted_iota(jnp.int32, (1, count), 1)
        labels = jnp.zeros((1, count), jnp.int32)
        sums = jnp.zeros((1, count), jnp.float32)
        for j in range((count + NV - 1) // NV + 1):
            offset = j * NV - start
            turned = pltpu.roll(table[...], (offset + TABLE) % TABLE, 1)[:, :count]
            inside = (lane >= offset) & (lane < offset + NV)
            labels = jnp.where(inside, turned[0:1].astype(jnp.int32) ^ irrep[head + j], labels)
            sums = jnp.where(inside, turned[1:2] + energy[head + j], sums)
        return labels.astype(jnp.float32), sums

    def denominators(out, sums, first):
        for r in range(out.shape[0]):
            out[r : r + 1, :] = sums - (occ[pairs[0, first + r]] + occ[pairs[1, first + r]])

    table[...] = jnp.zeros_like(table)
    table[0:1, :NV] = irreps[...].astype(jnp.float32)
    table[1:2, :NV] = energies[...]
    row, sums = window(place[0], place[1], rows_dev)
    denominators(den_ab, sums, place[4])
    col, sums = window(place[2], place[3], cols_dev)
    denominators(den_cd, sums, place[5])
    leaving = []
    for j, part in enumerate(parts):
        span = slice(j * TILE, (j + 1) * TILE)
        down = jnp.transpose(jnp.broadcast_to(row[:, span], (LANES, TILE)))
        part.wait()
        for c in range(cols_dev // LANES):
            lanes = slice(c * LANES, (c + 1) * LANES)
            label = jnp.where(tile_mask[j, c * LANES // TILE] == 1, col[:, lanes], -1.0)
            block = held[span, lanes].astype(jnp.float32)
            kept[span, lanes] = jnp.where(down == label, block, 0.0).astype(kept.dtype)
        leaving.append(pltpu.make_async_copy(kept.at[span, :], masked.at[span, :], stored.at[j]))
        leaving[-1].start()
    for part in leaving:
        part.wait()


def pick(choose, amps, chosen):
    for c in range(0, amps.shape[1], TILE):
        part = jnp.dot(choose[...], amps[:, c : c + TILE], preferred_element_type=jnp.float32)
        chosen[:, c : c + TILE] = part.astype(chosen.dtype)


def ab_kernel(groups, used, choose, amps, masked, coded, chosen, held, arrived):
    parts = copies(masked, held, arrived, 0)
    pick(choose, amps, chosen)
    for j, part in enumerate(parts):
        part.wait()
        span = slice(j * TILE, (j + 1) * TILE)
        sums = lax.dot_general(
            chosen[...], held[span, :], (((1,), (1,)), ((), ())), preferred_element_type=jnp.float32
        )
        rows, columns = sums.shape
        sums = sums.reshape(groups, rows // groups, columns)
        largest = jnp.max(jnp.abs(sums), axis=1, keepdims=True)
        scale = jnp.ceil(jnp.log2(jnp.maximum(largest, 2.0**-120)) * 256.0)
        whole = jnp.floor(sums * jnp.exp2(scale * (-1.0 / 256.0)) * 32767.0 + 0.5)
        place = lax.broadcasted_iota(jnp.int32, sums.shape, 1)
        whole = jnp.clip(jnp.where(place == used, scale, whole), -32767.0, 32767.0)
        coded[:, span] = whole.reshape(rows, columns).astype(jnp.int32).astype(jnp.int16)


def cd_kernel(choose, amps, masked, keep, give, chosen):
    rows, side = chosen.shape[0], amps.shape[1]

    @pl.when(pl.program_id(0) == 0)
    def _():
        for c in range(0, side, TILE):
            part = jnp.dot(choose[...], amps[:, c : c + TILE], preferred_element_type=jnp.float32)
            chosen[:, c : c + TILE] = part[:rows].astype(chosen.dtype)
            chosen[:, side + c : side + c + TILE] = part[rows:].astype(chosen.dtype)

    sums = jnp.dot(chosen[...], masked[...], preferred_element_type=jnp.float32)
    half = keep.shape[0]
    keep[...] = sums[:half]
    give[...] = sums[half:]


def decode_sum(coded, rows):
    scale = jnp.exp2(coded[:, rows : rows + 1].astype(jnp.float32) * (1.0 / 256.0)) * (1.0 / 32767.0)
    return jnp.sum(coded[:, :rows].astype(jnp.float32) * scale, axis=0)


def local(integrals, tile_mask, virt_irrep, occ_pairs, virt_energy, occ_energy, amp_ab, amp_cd):
    rows_dev = integrals.shape[0]
    cols_dev = integrals.shape[1]
    nzl, nx, ncore, ny, nzh = (lax.axis_size(a) for a in ("zl", "x", "core", "y", "zh"))
    zl, x, core, y, zh = (lax.axis_index(a) for a in ("zl", "x", "core", "y", "zh"))
    row_group = (zl * nx + x) * ncore + core
    col_group = y * nzh + zh
    nab = rows_dev * nzl * nx * ncore
    cd_count = amp_cd.shape[0]
    ab_count = amp_ab.shape[0]
    y_rows = nzh * ab_count
    y_pad = 40
    x_rows = nzl * cd_count
    x_pad = 40
    ab_rows = ny * y_pad
    cd_rows = ncore * nx * x_pad
    params = pltpu.CompilerParams(vmem_limit_bytes=VMEM_LIMIT)

    count = nzl * nx * ncore * 8
    half = cd_rows // ncore

    def ab_chooser():
        out = jnp.arange(ab_rows, dtype=jnp.int32)
        r = out % y_pad
        to_zh = (zh + 1 + r // ab_count) % nzh
        k = ((out // y_pad) * nzh + to_zh) * ab_count + r % ab_count
        group = k // cd_count
        source = ((group % (nx * ncore)) * nzl + group // (nx * ncore)) * 8 + k % cd_count
        return chooser(jnp.where(r < y_rows, source, -1), count)

    def cd_chooser():
        out = jnp.arange(cd_rows, dtype=jnp.int32)
        r = out % x_pad
        to_x = (x + out // x_pad) % nx
        to_core = (core + out // (x_pad * nx)) % ncore
        k = ((r // cd_count * nx + to_x) * ncore + to_core) * cd_count + r % cd_count
        source = k // y_rows * 2 * y_rows + k % y_rows
        source = jnp.concatenate([jnp.where(r < x_rows, source + part, -1) for part in (0, y_rows)])
        return chooser(source, 2 * ny * y_rows)

    other = send(amp_ab, "zh", shift(nzh, 1))
    first = jnp.where(zh == 0, amp_ab, other)
    second = jnp.where(zh == 0, other, amp_ab)
    side = rows_dev // 2
    both = jnp.concatenate([first[:, :side], second[:, :side], first[:, side:], second[:, side:]], axis=0)
    both = copied(both, ny)

    own = jnp.pad(copied(amp_cd, nzl), ((0, 0), (0, 8 - cd_count), (0, 0)))
    own = lax.all_to_all(own, "zl", 0, 0).reshape(nzl * 8, cols_dev)

    row_first = row_group * rows_dev
    col_first = nab + col_group * cols_dev
    place = jnp.stack(
        [row_first % NV, row_first // NV, col_first % NV, col_first // NV, col_group * ab_count, row_group * cd_count]
    ).astype(jnp.int32)
    smem = pl.BlockSpec(memory_space=pltpu.SMEM)
    vmem = pl.BlockSpec(memory_space=pltpu.VMEM)
    masked, den_ab, den_cd = pl.pallas_call(
        masked_kernel,
        in_specs=[smem] * 6 + [vmem, vmem, pl.BlockSpec(memory_space=pl.ANY)],
        out_specs=[pl.BlockSpec(memory_space=pl.ANY), vmem, vmem],
        out_shape=[
            jax.ShapeDtypeStruct(integrals.shape, integrals.dtype),
            jax.ShapeDtypeStruct((ab_count, rows_dev), jnp.float32),
            jax.ShapeDtypeStruct((cd_count, cols_dev), jnp.float32),
        ],
        scratch_shapes=[
            pltpu.VMEM((8, TABLE), jnp.float32),
            pltpu.VMEM(integrals.shape, integrals.dtype),
            pltpu.VMEM(integrals.shape, integrals.dtype),
            pltpu.SemaphoreType.DMA((rows_dev // TILE,)),
            pltpu.SemaphoreType.DMA((rows_dev // TILE,)),
        ],
        compiler_params=pltpu.CompilerParams(vmem_limit_bytes=MASK_LIMIT),
        cost_estimate=pl.CostEstimate(flops=4 * rows_dev * cols_dev, bytes_accessed=4 * rows_dev * cols_dev, transcendentals=0),
        name="masked",
    )(
        place,
        tile_mask,
        virt_irrep,
        virt_energy,
        occ_pairs,
        occ_energy,
        virt_irrep.reshape(1, NV),
        virt_energy.reshape(1, NV),
        integrals,
    )

    choose_ab, choose_cd = ab_chooser(), cd_chooser()
    own, masked, both, choose_ab = lax.optimization_barrier((own, masked, both, choose_ab))
    all_cd = lax.all_gather(own, ("x", "core"), axis=0, tiled=True)
    all_ab = lax.all_to_all(both, "y", 0, 0).reshape(2 * ny * y_rows, side)

    coded = pl.pallas_call(
        functools.partial(ab_kernel, ny, y_rows),
        in_specs=[vmem, vmem, pl.BlockSpec(memory_space=pl.ANY)],
        out_specs=vmem,
        out_shape=jax.ShapeDtypeStruct((ab_rows, rows_dev), jnp.int16),
        scratch_shapes=[
            pltpu.VMEM((ab_rows, cols_dev), jnp.bfloat16),
            pltpu.VMEM((rows_dev, cols_dev), jnp.bfloat16),
            pltpu.SemaphoreType.DMA((rows_dev // TILE,)),
        ],
        compiler_params=params,
        cost_estimate=pl.CostEstimate(
            flops=2 * ab_rows * cols_dev * (rows_dev + count), bytes_accessed=2 * rows_dev * cols_dev, transcendentals=0
        ),
        name="ab_product",
    )(choose_ab, all_cd, masked)

    all_ab, coded = lax.optimization_barrier((all_ab, coded))
    keep, give = pl.pallas_call(
        cd_kernel,
        grid=(cols_dev // TILE,),
        in_specs=[
            pl.BlockSpec((2 * cd_rows, 2 * ny * y_rows), lambda i: (0, 0)),
            pl.BlockSpec((2 * ny * y_rows, side), lambda i: (0, 0)),
            pl.BlockSpec((rows_dev, TILE), lambda i: (0, i)),
        ],
        out_specs=[pl.BlockSpec((half, TILE), lambda i: (0, i))] * 2,
        out_shape=[jax.ShapeDtypeStruct((half, cols_dev), jnp.float32)] * 2,
        scratch_shapes=[pltpu.VMEM((cd_rows, rows_dev), jnp.bfloat16)],
        compiler_params=params,
        cost_estimate=pl.CostEstimate(
            flops=2 * cd_rows * rows_dev * (cols_dev + ab_rows), bytes_accessed=2 * rows_dev * cols_dev, transcendentals=0
        ),
        name="cd_product",
    )(choose_cd, all_ab, masked)

    coded = lax.all_to_all(coded.reshape(ny, y_pad, rows_dev), "y", 0, 0)

    total = keep + send(give, "core", shift(ncore, 1))
    total = total.reshape(nx, x_pad, cols_dev)
    near, far, back = (send(total[t], "x", shift(nx, t)) for t in range(1, nx))
    coded, near = lax.optimization_barrier((coded, near))
    total_ab = decode_sum(coded, y_rows)
    ladder_ab = total_ab[ab_count:] + send(total_ab[:ab_count], "zh", shift(nzh, 1))
    total = (total[0] + near) + (far + back)
    total = total[:x_rows].reshape(nzl, cd_count, cols_dev)
    ladder_cd = jnp.sum(lax.all_to_all(total, "zl", 0, 0), axis=0)
    return (ladder_ab / den_ab, ladder_cd / den_cd)


def solution(mesh):
    fine = Mesh(mesh.devices.reshape(6, 4, 2, 8, 2), AB + CD)
    return jax.shard_map(
        local,
        mesh=fine,
        in_specs=(P(AB, CD), P(AB, CD), P(), P(), P(), P(), P(CD, AB), P(AB, CD)),
        out_specs=(P(CD, AB), P(AB, CD)),
        check_vma=False,
    )
```
